32 devices in a mesh: crop: 2 (over y), row: 4 (over z), chan: 2 (over x), sub: 2 (over core).
Axes of the slice: x: 2, y: 2, z: 4, core: 2. Of those that a mesh axis runs over, the one named last changes fastest.
Arguments:
- pair_state: bfloat16 [192, 96, 128], P(('crop', 'row'), ('chan', 'sub')), parts along dimension 0, may hold values from -6 to 6
- chain_lengths: int32 [8], P('crop'), parts along dimension 0, may hold values from 1 to 24, 72 in all
- proj_weights: bfloat16 [2, 128, 640], replicated, may hold values from -0.5 to 0.5
- out_weights: bfloat16 [2, 128, 128], replicated, may hold values from -0.5 to 0.5
- input_gains: float32 [2, 128], replicated, may hold values from 0.25 to 1.75
- output_gains: float32 [2, 128], replicated, may hold values from 0.25 to 1.75
Outputs:
- updated_pair: bfloat16 [192, 96, 128], P(('crop', 'row'), ('chan', 'sub')), parts along dimension 0
The draws below stay inside these ranges and needn't reach their ends.
There are 2 independent parts, one for each index of `crop`. The reference program is written for one: setup_inputs(seed, part) draws one part's arguments, and reference() takes and returns one part's arrays. A program takes and returns all parts, laid end to end along the dimension named above; an argument that names none is the same for every part. Nothing has to cross between parts.
Inputs may be any that keep to these rules, and one draw needn't show every extreme that they name: Chain slot s covers residues s * 24 to (s + 1) * 24 - 1, of which the first chain_lengths[s] are valid; the lengths sum to 72 and one of them equals 24.
All inputs are finite; a program needn't handle non-finite values.
Results may differ from the reference program's by a relative error of at most 0.01.
Values may be sent and summed in bfloat16 or wider, within the bound.
A program may use at most 64 MiB of HBM per device.

```python
import math
import jax
import jax.numpy as jnp
import numpy as np
from jax import lax

CZ = 128
C = 128
CHAINS = 4
N = 96
SLOT = 24


def steps_of(key, shape, split, smallest, high):
    def one(position, shards_of):
        heights = jax.random.uniform(jax.random.fold_in(jax.random.fold_in(key, 6), position), (shards_of,), jnp.float32, smallest / len(split), high / len(split))
        return jnp.repeat(jnp.exp(heights), shape[position] // shards_of).reshape((-1,) + (1,) * (len(shape) - position - 1))

    gain = one(*split[0])
    for cut in split[1:]:
        gain = gain * one(*cut)
    return gain


def split_up(count, total, limit, slope):
    weights = [(1 << 20) // math.isqrt(grade ** slope) + 1 for grade in range(2, count + 1)]
    rest, given = total - limit - (count - 1), [1] * (count - 1)
    while rest > 0:
        free = [i for i in range(count - 1) if given[i] < limit]
        mass, budget = sum([weights[i] for i in free]), rest
        for i in free:
            addition = min(limit - given[i], max(1, budget * weights[i] // mass), rest)
            given[i] = given[i] + addition
            rest = rest - addition
    return np.array([limit] + given)


def uneven(rng, count, total, most, slope):
    if count == 2:
        one = jax.random.randint(rng, (), max(1, total - most), min(most, total - 1) + 1)
        return jnp.stack([one, total - one])
    sizes = jnp.asarray(split_up(count, total, most, slope), jnp.int32)
    pairs = (count - 1) // 2
    giver, taker = sizes[1:1 + 2 * pairs:2], sizes[2:2 + 2 * pairs:2]
    slack = jnp.minimum(giver - 1, most - taker)
    moved = jax.random.randint(jax.random.fold_in(rng, 1), (pairs,), 0, 1 << 20) % (slack + 1)
    sizes = sizes.at[1:1 + 2 * pairs:2].set(giver - moved).at[2:2 + 2 * pairs:2].set(taker + moved)
    return sizes[jax.random.permutation(jax.random.fold_in(rng, 2), count)]


def gaussian(own_key, dims, scale, bound, split=(), kind=jnp.bfloat16):
    values = jax.random.normal(own_key, dims, jnp.float32) * scale
    if len(split) > 0:
        values = steps_of(own_key, dims, split, -0.22, 0.18) * values
    return jnp.clip(values, min=-bound, max=bound).astype(kind)


def setup_inputs(seed: int = 0, part: int = 0) -> dict:
    arg_keys = jax.random.split(jax.random.key(seed), 7)
    own_keys = jax.random.split(jax.random.fold_in(arg_keys[6], part), 7)
    pair_state = gaussian(own_keys[0], (N, N, CZ), 1.0, 6.0, ((0, 4), (1, 4)))
    chain_lengths = uneven(own_keys[1], CHAINS, 3 * SLOT, SLOT, 0).astype(jnp.int32)
    proj_weights = gaussian(arg_keys[2], (2, CZ, 4 * C + CZ), CZ ** -0.5, 0.5)
    out_weights = gaussian(arg_keys[3], (2, C, CZ), C ** -0.5, 0.5)
    input_gains = jnp.clip(1.0 + 0.15 * jax.random.normal(arg_keys[4], (2, CZ), jnp.float32), 0.25, 1.75)
    output_gains = jnp.clip(1.0 + 0.15 * jax.random.normal(arg_keys[5], (2, C), jnp.float32), 0.25, 1.75)
    return dict(pair_state=pair_state, chain_lengths=chain_lengths, proj_weights=proj_weights, out_weights=out_weights, input_gains=input_gains, output_gains=output_gains)


epsilon = 1e-05

def layer_norm(values, gains):
    values = values.astype(jnp.float32)
    average = lax.optimization_barrier(jnp.mean(values, axis=-1, keepdims=True))
    centred = values - average
    variance = lax.optimization_barrier(jnp.mean(centred * centred, axis=-1, keepdims=True))
    return centred * lax.rsqrt(variance + epsilon) * gains.astype(jnp.float32)

def residue_valid(chain_lengths):
    positions = jnp.arange(N, dtype=jnp.int32)
    limits = chain_lengths[(positions // SLOT).astype(jnp.int32)]
    return (positions % SLOT < limits).astype(jnp.float32)

def triangle(source, valid, weights_in, weights_out, gains_in, gains_out, incoming):

    def edges(items):
        row_values, row_valid = items
        normed = layer_norm(row_values, gains_in).astype(jnp.bfloat16)
        projected = jnp.dot(normed, weights_in[:, :4 * C], preferred_element_type=jnp.float32)
        row_mask = (row_valid * valid)[:, None]
        left_edges = (row_mask * jax.nn.sigmoid(projected[:, C:2 * C]) * projected[:, :C]).astype(jnp.bfloat16)
        right_edges = (row_mask * jax.nn.sigmoid(projected[:, 3 * C:4 * C]) * projected[:, 2 * C:3 * C]).astype(jnp.bfloat16)
        return (left_edges.T, right_edges.T)
    left_edges, right_edges = lax.map(edges, (source, valid))
    left_edges = jnp.transpose(left_edges, (1, 0, 2))
    right_edges = jnp.transpose(right_edges, (1, 0, 2))

    def channel(items):
        first, second = items
        if incoming:
            return jnp.dot(first.T, second, preferred_element_type=jnp.float32).astype(jnp.bfloat16)
        return jnp.dot(first, second.T, preferred_element_type=jnp.float32).astype(jnp.bfloat16)
    product = lax.map(channel, (left_edges, right_edges))
    product = jnp.transpose(product, (1, 2, 0))

    def finish(items):
        row_values, product_row = items
        normed = layer_norm(row_values, gains_in).astype(jnp.bfloat16)
        gate_value = jax.nn.sigmoid(jnp.dot(normed, weights_in[:, 4 * C:], preferred_element_type=jnp.float32))
        renormed = layer_norm(product_row, gains_out).astype(jnp.bfloat16)
        update = gate_value * jnp.dot(renormed, weights_out, preferred_element_type=jnp.float32)
        return (row_values.astype(jnp.float32) + update).astype(jnp.bfloat16)
    return lax.map(finish, (source, product))

def reference(pair_state, chain_lengths, proj_weights, out_weights, input_gains, output_gains):
    valid = residue_valid(chain_lengths)
    middle = triangle(pair_state, valid, proj_weights[0], out_weights[0], input_gains[0], output_gains[0], False)
    return triangle(middle, valid, proj_weights[1], out_weights[1], input_gains[1], output_gains[1], True)
```

```python
import functools

import jax
import jax.numpy as jnp
from jax import lax
from jax.experimental import pallas as pl
from jax.experimental.pallas import tpu as pltpu
from jax.sharding import PartitionSpec as P

MESH = pl.DeviceIdType.MESH
epsilon = 1e-05
f32 = jnp.float32
bf16 = jnp.bfloat16


def layer_norm(values, gains):
    average = jnp.mean(values, axis=-1, keepdims=True)
    centred = values - average
    variance = jnp.mean(centred * centred, axis=-1, keepdims=True)
    return centred * lax.rsqrt(variance + epsilon) * gains


def valid_at(lengths_ref, positions, slot):
    valid = jnp.zeros(positions.shape, f32)
    for chain in range(lengths_ref.shape[0]):
        first = chain * slot
        inside = (positions >= first) & (positions < first + lengths_ref[chain])
        valid = jnp.where(inside, 1.0, valid)
    return valid


def partial_product(left_ref, right, depth, store):
    count = left_ref.shape[1]

    def block(b, carry):
        first = pl.multiple_of(b * 8, 8)

        def step(k, sums):
            other = right(k)
            return tuple(
                total + left_ref[k, pl.ds(first + n, 1), :] * other
                for n, total in enumerate(sums)
            )

        zero = jnp.zeros(right(0).shape, f32)
        sums = lax.fori_loop(0, depth, step, (zero,) * 8, unroll=8)
        for n, total in enumerate(sums):
            store(first + n, total)
        return carry

    lax.fori_loop(0, count // 8, block, 0)


def kernel(
    rows_n, chans, subs, slot,
    x_ref, lengths_ref, w_ref, wo_ref, gi_ref, go_ref, out_ref,
    left, right, gate, mid, total,
    r_send, r_recv, p_send, p_recv, l_send, l_recv, q_send, q_recv,
    r_ssem, r_rsem, p_ssem, p_rsem, l_ssem, l_rsem, q_ssem, q_rsem,
):
    rows, cols, feat = x_ref.shape
    cols_n = chans * subs
    per_col = cols // rows
    row = lax.axis_index("row")
    chan, sub = lax.axis_index("chan"), lax.axis_index("sub")
    col = chan * subs + sub

    def in_row(other):
        return {"chan": other // subs, "sub": lax.rem(other, subs)}

    barrier = pltpu.get_barrier_semaphore()
    for t in range(1, rows_n):
        pl.semaphore_signal(
            barrier, inc=1, device_id={"row": lax.rem(row + t, rows_n)}, device_id_type=MESH
        )
    for t in range(1, cols_n):
        pl.semaphore_signal(
            barrier, inc=1, device_id=in_row(lax.rem(col + t, cols_n)), device_id_type=MESH
        )

    def positions(start, shape, axis):
        return start + lax.broadcasted_iota(jnp.int32, shape, axis)

    row_lead = valid_at(lengths_ref, positions(row * rows, (rows, 1, feat), 0), slot)
    col_lead = valid_at(lengths_ref, positions(col * cols, (cols, 1, feat), 0), slot)
    row_line = valid_at(lengths_ref, positions(row * rows, (1, rows, feat), 1), slot)
    col_line = valid_at(lengths_ref, positions(col * cols, (1, cols, feat), 1), slot)

    def edges(normed, mask, module, first):
        both = jnp.dot(
            normed, w_ref[module, :, first : first + 2 * feat], preferred_element_type=f32
        )
        return mask * jax.nn.sigmoid(both[:, feat:]) * both[:, :feat]

    def flat(values):
        return values.reshape(values.shape[0] * values.shape[1], values.shape[2])

    def copy(source, target, send, receive, device):
        return pltpu.make_async_remote_copy(
            src_ref=source, dst_ref=target, send_sem=send, recv_sem=receive,
            device_id=device, device_id_type=MESH,
        )

    source = flat(x_ref[...].astype(f32))
    normed = layer_norm(source, gi_ref[0:1, :])
    turned = flat(jnp.swapaxes(normed.reshape(rows, cols, feat), 0, 1)).astype(bf16)
    mask = flat(col_lead * row_line)
    right_now = edges(turned, mask, 0, 2 * feat).astype(bf16)
    r_send[...] = right_now
    pl.semaphore_wait(barrier, rows_n + cols_n - 2)

    def r_copy(t):
        other = lax.rem(row + t, rows_n)
        return copy(r_send, r_recv.at[row], r_ssem.at[other], r_rsem.at[row], {"row": other})

    for t in range(1, rows_n):
        r_copy(t).start()
    right[: cols, : rows, :] = right_now.astype(f32).reshape(cols, rows, feat)
    left[: cols, : rows, :] = (
        edges(turned, mask, 0, 0).astype(bf16).astype(f32).reshape(cols, rows, feat)
    )
    gate[...] = jax.nn.sigmoid(
        jnp.dot(normed.astype(bf16), w_ref[0, :, 4 * feat :], preferred_element_type=f32)
    )

    def p_copy(other):
        owner, place = other // per_col, lax.rem(other, per_col)
        return copy(
            p_send.at[other], p_recv.at[col, place], p_ssem.at[other],
            p_rsem.at[col, place], in_row(owner),
        )

    for t in range(rows_n):
        other = lax.rem(row + t, rows_n)
        if t > 0:
            copy(
                r_send, r_recv.at[other], r_ssem.at[other], r_rsem.at[other], {"row": other}
            ).wait_recv()
            right[: cols, : rows, :] = r_recv[other].astype(f32).reshape(cols, rows, feat)

        def store(i, value):
            total[pl.ds(pl.multiple_of(i * rows, 8), rows), :] = value

        partial_product(
            left.at[: cols, : rows, :], lambda k: right[k, : rows, :], cols, store
        )
        owner, place = other // per_col, lax.rem(other, per_col)
        p_send[other] = total[: rows * rows, :].astype(bf16)

        @pl.when(owner != col)
        def _():
            p_copy(other).start()

        @pl.when(owner == col)
        def _():
            p_recv[col, place] = p_send[other]

    pieces = []
    for place in range(per_col):
        pieces.append(p_recv[col, place].astype(f32))
    for t in range(1, cols_n):
        other = lax.rem(col + t, cols_n)
        for place in range(per_col):
            copy(
                p_send.at[0], p_recv.at[other, place], p_ssem.at[0],
                p_rsem.at[other, place], in_row(other),
            ).wait_recv()
            pieces[place] += p_recv[other, place].astype(f32)
    product = jnp.concatenate(
        [piece.reshape(rows, rows, feat) for piece in pieces], axis=1
    )
    product = flat(product)

    def finish(product, source, module):
        renormed = layer_norm(product, go_ref[module : module + 1, :]).astype(bf16)
        update = gate[...] * jnp.dot(renormed, wo_ref[module], preferred_element_type=f32)
        return (source + update).astype(bf16)

    middle = finish(product, flat(x_ref[...].astype(f32)), 0).astype(f32)
    mid[...] = middle

    normed = layer_norm(middle, gi_ref[1:2, :]).astype(bf16)
    mask = flat(row_lead * col_line)
    left_now = edges(normed, mask, 1, 0).astype(bf16)
    l_send[...] = left_now

    def l_copy(t):
        other = lax.rem(col + t, cols_n)
        return copy(l_send, l_recv.at[col], l_ssem.at[other], l_rsem.at[col], in_row(other))

    for t in range(1, cols_n):
        l_copy(t).start()
    left[: rows, : cols, :] = left_now.astype(f32).reshape(rows, cols, feat)
    right[: rows, : cols, :] = (
        edges(normed, mask, 1, 2 * feat).astype(bf16).astype(f32).reshape(rows, cols, feat)
    )

    def q_copy(block):
        return copy(
            q_send.at[block], q_recv.at[row], q_ssem.at[block], q_rsem.at[row], {"row": block}
        )

    for t in range(cols_n):
        other = lax.rem(col + t, cols_n)
        if t > 0:
            copy(
                l_send, l_recv.at[other], l_ssem.at[other], l_rsem.at[other], in_row(other)
            ).wait_recv()
            left[: rows, : cols, :] = l_recv[other].astype(f32).reshape(rows, cols, feat)

        def store(i, value):
            total[pl.ds(pl.multiple_of(i * cols, 8), cols), :] = value

        partial_product(
            left.at[: rows, : cols, :], lambda k: right[k, : cols, :], rows, store
        )
        for place in range(per_col):
            block = other * per_col + place
            size = rows * cols
            q_send[block] = total[place * size : (place + 1) * size, :].astype(bf16)

            @pl.when(block != row)
            def _():
                q_copy(block).start()

            @pl.when(block == row)
            def _():
                q_recv[row] = q_send[block]

        if t == 0:
            gate[...] = jax.nn.sigmoid(
                jnp.dot(normed, w_ref[1, :, 4 * feat :], preferred_element_type=f32)
            )

    product = q_recv[row].astype(f32)
    for t in range(1, rows_n):
        other = lax.rem(row + t, rows_n)
        copy(
            q_send.at[0], q_recv.at[other], q_ssem.at[0], q_rsem.at[other], {"row": other}
        ).wait_recv()
        product += q_recv[other].astype(f32)
    out_ref[...] = finish(product, mid[...], 1).astype(f32).reshape(rows, cols, feat).astype(bf16)

    for t in range(1, rows_n):
        r_copy(t).wait_send()
    for t in range(1, cols_n):
        l_copy(t).wait_send()
    for other in range(rows_n):

        @pl.when(other // per_col != col)
        def _():
            p_copy(other).wait_send()

        @pl.when(other != row)
        def _():
            q_copy(other).wait_send()


def solution(mesh):
    rows_n, chans, subs = mesh.shape["row"], mesh.shape["chan"], mesh.shape["sub"]
    cols_n = chans * subs

    def body(pair_state, chain_lengths, proj_weights, out_weights, input_gains, output_gains):
        rows, cols, feat = pair_state.shape
        slot = rows * rows_n // chain_lengths.shape[0]
        per_col = cols // rows
        pairs = rows * cols
        vmem = pl.BlockSpec(memory_space=pltpu.VMEM)
        dma = pltpu.SemaphoreType.DMA
        return pl.pallas_call(
            functools.partial(kernel, rows_n, chans, subs, slot),
            out_shape=jax.ShapeDtypeStruct(pair_state.shape, bf16),
            in_specs=[vmem, pl.BlockSpec(memory_space=pltpu.SMEM)] + [vmem] * 4,
            out_specs=vmem,
            scratch_shapes=[
                pltpu.VMEM((cols, cols, feat), f32),
                pltpu.VMEM((cols, cols, feat), f32),
                pltpu.VMEM((pairs, feat), f32),
                pltpu.VMEM((pairs, feat), f32),
                pltpu.VMEM((cols * cols, feat), f32),
                pltpu.VMEM((pairs, feat), bf16),
                pltpu.VMEM((rows_n, pairs, feat), bf16),
                pltpu.VMEM((rows_n, rows * rows, feat), bf16),
                pltpu.VMEM((cols_n, per_col, rows * rows, feat), bf16),
                pltpu.VMEM((pairs, feat), bf16),
                pltpu.VMEM((cols_n, pairs, feat), bf16),
                pltpu.VMEM((rows_n, pairs, feat), bf16),
                pltpu.VMEM((rows_n, pairs, feat), bf16),
                dma((rows_n,)), dma((rows_n,)),
                dma((rows_n,)), dma((cols_n, per_col)),
                dma((cols_n,)), dma((cols_n,)),
                dma((rows_n,)), dma((rows_n,)),
            ],
            compiler_params=pltpu.CompilerParams(
                collective_id=0, has_side_effects=True, vmem_limit_bytes=48 * 1024 * 1024
            ),
        )(pair_state, chain_lengths, proj_weights, out_weights, input_gains, output_gains)

    placed = (P(("crop", "row"), ("chan", "sub"), None), P("crop"), P(), P(), P(), P())
    return jax.shard_map(
        body,
        mesh=mesh,
        in_specs=placed,
        out_specs=P(("crop", "row"), ("chan", "sub"), None),
        check_vma=False,
    )
```

```python
import functools

import jax
import jax.numpy as jnp
from jax import lax
from jax.experimental import pallas as pl
from jax.experimental.pallas import tpu as pltpu
from jax.sharding import PartitionSpec as P

MESH = pl.DeviceIdType.MESH
epsilon = 1e-05
f32 = jnp.float32
bf16 = jnp.bfloat16


def layer_norm(values, gains):
    average = jnp.mean(values, axis=-1, keepdims=True)
    centred = values - average
    variance = jnp.mean(centred * centred, axis=-1, keepdims=True)
    return centred * lax.rsqrt(variance + epsilon) * gains


def valid_at(lengths_ref, positions, slot):
    valid = jnp.zeros(positions.shape, f32)
    for chain in range(lengths_ref.shape[0]):
        first = chain * slot
        inside = (positions >= first) & (positions < first + lengths_ref[chain])
        valid = jnp.where(inside, 1.0, valid)
    return valid


def partial_product(left_ref, right, depth, store):
    count = left_ref.shape[1]

    def block(b, carry):
        first = pl.multiple_of(b * 8, 8)

        def step(k, sums):
            other = right(k)
            return tuple(
                total + left_ref[k, pl.ds(first + n, 1), :] * other
                for n, total in enumerate(sums)
            )

        zero = jnp.zeros(right(0).shape, f32)
        sums = lax.fori_loop(0, depth, step, (zero,) * 8, unroll=8)
        for n, total in enumerate(sums):
            store(first + n, total)
        return carry

    lax.fori_loop(0, count // 8, block, 0)


def kernel(
    rows_n, chans, subs, slot,
    x_hbm, lengths_hbm, w_hbm, wo_hbm, gi_hbm, go_hbm, out_ref,
    x_ref, lengths_ref, w_ref, wo_ref, gi_ref, go_ref, load_sem,
    left, right, gate, mid, total,
    r_send, r_recv, p_send, p_recv, l_send, l_recv, q_send, q_recv,
    r_ssem, r_rsem, p_ssem, p_rsem, l_ssem, l_rsem, q_ssem, q_rsem,
):
    loads = [
        pltpu.make_async_copy(source, target, load_sem.at[n])
        for n, (source, target) in enumerate(
            [
                (x_hbm, x_ref), (gi_hbm, gi_ref), (lengths_hbm, lengths_ref),
                (w_hbm, w_ref), (go_hbm, go_ref), (wo_hbm, wo_ref),
            ]
        )
    ]
    for load in loads:
        load.start()
    rows, cols, feat = x_ref.shape
    cols_n = chans * subs
    per_col = cols // rows
    row = lax.axis_index("row")
    chan, sub = lax.axis_index("chan"), lax.axis_index("sub")
    col = chan * subs + sub

    def in_row(other):
        return {"chan": other // subs, "sub": lax.rem(other, subs)}

    barrier = pltpu.get_barrier_semaphore()
    for t in range(1, rows_n):
        pl.semaphore_signal(
            barrier, inc=1, device_id={"row": lax.rem(row + t, rows_n)}, device_id_type=MESH
        )
    for t in range(1, cols_n):
        pl.semaphore_signal(
            barrier, inc=1, device_id=in_row(lax.rem(col + t, cols_n)), device_id_type=MESH
        )

    loads[2].wait()

    def positions(start, shape, axis):
        return start + lax.broadcasted_iota(jnp.int32, shape, axis)

    row_lead = valid_at(lengths_ref, positions(row * rows, (rows, 1, feat), 0), slot)
    col_lead = valid_at(lengths_ref, positions(col * cols, (cols, 1, feat), 0), slot)
    row_line = valid_at(lengths_ref, positions(row * rows, (1, rows, feat), 1), slot)
    col_line = valid_at(lengths_ref, positions(col * cols, (1, cols, feat), 1), slot)

    def edges(normed, mask, module, first):
        both = jnp.dot(
            normed, w_ref[module, :, first : first + 2 * feat], preferred_element_type=f32
        )
        return mask * jax.nn.sigmoid(both[:, feat:]) * both[:, :feat]

    def flat(values):
        return values.reshape(values.shape[0] * values.shape[1], values.shape[2])

    def copy(source, target, send, receive, device):
        return pltpu.make_async_remote_copy(
            src_ref=source, dst_ref=target, send_sem=send, recv_sem=receive,
            device_id=device, device_id_type=MESH,
        )

    loads[0].wait()
    loads[1].wait()
    source = flat(x_ref[...].astype(f32))
    normed = layer_norm(source, gi_ref[0:1, :])
    turned = flat(jnp.swapaxes(normed.reshape(rows, cols, feat), 0, 1)).astype(bf16)
    mask = flat(col_lead * row_line)
    loads[3].wait()
    right_now = edges(turned, mask, 0, 2 * feat).astype(bf16)
    r_send[...] = right_now
    pl.semaphore_wait(barrier, rows_n + cols_n - 2)

    def r_copy(t):
        other = lax.rem(row + t, rows_n)
        return copy(r_send, r_recv.at[row], r_ssem.at[other], r_rsem.at[row], {"row": other})

    for t in range(1, rows_n):
        r_copy(t).start()
    right[: cols, : rows, :] = right_now.astype(f32).reshape(cols, rows, feat)
    left[: cols, : rows, :] = (
        edges(turned, mask, 0, 0).astype(bf16).astype(f32).reshape(cols, rows, feat)
    )
    gate[...] = jax.nn.sigmoid(
        jnp.dot(normed.astype(bf16), w_ref[0, :, 4 * feat :], preferred_element_type=f32)
    )

    def p_copy(other):
        owner, place = other // per_col, lax.rem(other, per_col)
        return copy(
            p_send.at[other], p_recv.at[col, place], p_ssem.at[other],
            p_rsem.at[col, place], in_row(owner),
        )

    for t in range(rows_n):
        other = lax.rem(row + t, rows_n)
        if t > 0:
            copy(
                r_send, r_recv.at[other], r_ssem.at[other], r_rsem.at[other], {"row": other}
            ).wait_recv()
            right[: cols, : rows, :] = r_recv[other].astype(f32).reshape(cols, rows, feat)

        def store(i, value):
            total[pl.ds(pl.multiple_of(i * rows, 8), rows), :] = value

        partial_product(
            left.at[: cols, : rows, :], lambda k: right[k, : rows, :], cols, store
        )
        owner, place = other // per_col, lax.rem(other, per_col)
        p_send[other] = total[: rows * rows, :].astype(bf16)

        @pl.when(owner != col)
        def _():
            p_copy(other).start()

        @pl.when(owner == col)
        def _():
            p_recv[col, place] = p_send[other]

    loads[4].wait()
    loads[5].wait()
    pieces = []
    for place in range(per_col):
        pieces.append(p_recv[col, place].astype(f32))
    for t in range(1, cols_n):
        other = lax.rem(col + t, cols_n)
        for place in range(per_col):
            copy(
                p_send.at[0], p_recv.at[other, place], p_ssem.at[0],
                p_rsem.at[other, place], in_row(other),
            ).wait_recv()
            pieces[place] += p_recv[other, place].astype(f32)
    product = jnp.concatenate(
        [piece.reshape(rows, rows, feat) for piece in pieces], axis=1
    )
    product = flat(product)

    def finish(product, source, module):
        renormed = layer_norm(product, go_ref[module : module + 1, :]).astype(bf16)
        update = gate[...] * jnp.dot(renormed, wo_ref[module], preferred_element_type=f32)
        return (source + update).astype(bf16)

    middle = finish(product, flat(x_ref[...].astype(f32)), 0).astype(f32)
    mid[...] = middle

    normed = layer_norm(middle, gi_ref[1:2, :]).astype(bf16)
    mask = flat(row_lead * col_line)
    left_now = edges(normed, mask, 1, 0).astype(bf16)
    l_send[...] = left_now

    def l_copy(t):
        other = lax.rem(col + t, cols_n)
        return copy(l_send, l_recv.at[col], l_ssem.at[other], l_rsem.at[col], in_row(other))

    for t in range(1, cols_n):
        l_copy(t).start()
    left[: rows, : cols, :] = left_now.astype(f32).reshape(rows, cols, feat)
    right[: rows, : cols, :] = (
        edges(normed, mask, 1, 2 * feat).astype(bf16).astype(f32).reshape(rows, cols, feat)
    )

    def q_copy(block):
        return copy(
            q_send.at[block], q_recv.at[row], q_ssem.at[block], q_rsem.at[row], {"row": block}
        )

    for t in range(cols_n):
        other = lax.rem(col + t, cols_n)
        if t > 0:
            copy(
                l_send, l_recv.at[other], l_ssem.at[other], l_rsem.at[other], in_row(other)
            ).wait_recv()
            left[: rows, : cols, :] = l_recv[other].astype(f32).reshape(rows, cols, feat)

        def store(i, value):
            total[pl.ds(pl.multiple_of(i * cols, 8), cols), :] = value

        partial_product(
            left.at[: rows, : cols, :], lambda k: right[k, : cols, :], rows, store
        )
        for place in range(per_col):
            block = other * per_col + place
            size = rows * cols
            q_send[block] = total[place * size : (place + 1) * size, :].astype(bf16)

            @pl.when(block != row)
            def _():
                q_copy(block).start()

            @pl.when(block == row)
            def _():
                q_recv[row] = q_send[block]

        if t == 0:
            gate[...] = jax.nn.sigmoid(
                jnp.dot(normed, w_ref[1, :, 4 * feat :], preferred_element_type=f32)
            )

    product = q_recv[row].astype(f32)
    for t in range(1, rows_n):
        other = lax.rem(row + t, rows_n)
        copy(
            q_send.at[0], q_recv.at[other], q_ssem.at[0], q_rsem.at[other], {"row": other}
        ).wait_recv()
        product += q_recv[other].astype(f32)
    out_ref[...] = finish(product, mid[...], 1).astype(f32).reshape(rows, cols, feat).astype(bf16)

    for t in range(1, rows_n):
        r_copy(t).wait_send()
    for t in range(1, cols_n):
        l_copy(t).wait_send()
    for other in range(rows_n):

        @pl.when(other // per_col != col)
        def _():
            p_copy(other).wait_send()

        @pl.when(other != row)
        def _():
            q_copy(other).wait_send()


def solution(mesh):
    rows_n, chans, subs = mesh.shape["row"], mesh.shape["chan"], mesh.shape["sub"]
    cols_n = chans * subs

    def body(pair_state, chain_lengths, proj_weights, out_weights, input_gains, output_gains):
        rows, cols, feat = pair_state.shape
        slot = rows * rows_n // chain_lengths.shape[0]
        per_col = cols // rows
        pairs = rows * cols
        vmem = pl.BlockSpec(memory_space=pltpu.VMEM)
        dma = pltpu.SemaphoreType.DMA
        return pl.pallas_call(
            functools.partial(kernel, rows_n, chans, subs, slot),
            out_shape=jax.ShapeDtypeStruct(pair_state.shape, bf16),
            in_specs=[pl.BlockSpec(memory_space=pl.ANY)] * 6,
            out_specs=vmem,
            scratch_shapes=[
                pltpu.VMEM(pair_state.shape, bf16),
                pltpu.SMEM(chain_lengths.shape, jnp.int32),
                pltpu.VMEM(proj_weights.shape, bf16),
                pltpu.VMEM(out_weights.shape, bf16),
                pltpu.VMEM(input_gains.shape, f32),
                pltpu.VMEM(output_gains.shape, f32),
                dma((6,)),
                pltpu.VMEM((cols, cols, feat), f32),
                pltpu.VMEM((cols, cols, feat), f32),
                pltpu.VMEM((pairs, feat), f32),
                pltpu.VMEM((pairs, feat), f32),
                pltpu.VMEM((cols * cols, feat), f32),
                pltpu.VMEM((pairs, feat), bf16),
                pltpu.VMEM((rows_n, pairs, feat), bf16),
                pltpu.VMEM((rows_n, rows * rows, feat), bf16),
                pltpu.VMEM((cols_n, per_col, rows * rows, feat), bf16),
                pltpu.VMEM((pairs, feat), bf16),
                pltpu.VMEM((cols_n, pairs, feat), bf16),
                pltpu.VMEM((rows_n, pairs, feat), bf16),
                pltpu.VMEM((rows_n, pairs, feat), bf16),
                dma((rows_n,)), dma((rows_n,)),
                dma((rows_n,)), dma((cols_n, per_col)),
                dma((cols_n,)), dma((cols_n,)),
                dma((rows_n,)), dma((rows_n,)),
            ],
            compiler_params=pltpu.CompilerParams(
                collective_id=0, has_side_effects=True, vmem_limit_bytes=60 * 1024 * 1024
            ),
        )(pair_state, chain_lengths, proj_weights, out_weights, input_gains, output_gains)

    placed = (P(("crop", "row"), ("chan", "sub"), None), P("crop"), P(), P(), P(), P())
    return jax.shard_map(
        body,
        mesh=mesh,
        in_specs=placed,
        out_specs=P(("crop", "row"), ("chan", "sub"), None),
        check_vma=False,
    )
```

```python
import functools

import jax
import jax.numpy as jnp
from jax import lax
from jax.experimental import pallas as pl
from jax.experimental.pallas import tpu as pltpu
from jax.sharding import PartitionSpec as P

MESH = pl.DeviceIdType.MESH
epsilon = 1e-05
f32 = jnp.float32
bf16 = jnp.bfloat16


def layer_norm(values, gains):
    average = jnp.mean(values, axis=-1, keepdims=True)
    centred = values - average
    variance = jnp.mean(centred * centred, axis=-1, keepdims=True)
    return centred * lax.rsqrt(variance + epsilon) * gains


def valid_at(lengths_ref, positions, slot):
    valid = jnp.zeros(positions.shape, f32)
    for chain in range(lengths_ref.shape[0]):
        first = chain * slot
        inside = (positions >= first) & (positions < first + lengths_ref[chain])
        valid = jnp.where(inside, 1.0, valid)
    return valid


def partial_product(left, right, depth, count, store):
    def step(k, sums):
        other = right(k)
        return tuple(total + left(k, i) * other for i, total in enumerate(sums))

    zero = jnp.zeros(right(0).shape, f32)
    sums = lax.fori_loop(0, depth, step, (zero,) * count, unroll=8)
    for i, total in enumerate(sums):
        store(i, total)


def kernel(
    rows_n, chans, subs, slot,
    x_hbm, lengths_hbm, w_hbm, wo_hbm, gi_hbm, go_hbm, out_ref,
    x_ref, lengths_ref, w_ref, wo_ref, gi_ref, go_ref, load_sem,
    left, right, part, gate, mid, total,
    r_send, r_recv, p_send, p_recv, p_own, l_send, l_recv, q_send, q_recv,
    r_ssem, r_rsem, p_ssem, p_rsem, l_ssem, l_rsem, q_ssem, q_rsem,
):
    loads = [
        pltpu.make_async_copy(source, target, load_sem.at[n])
        for n, (source, target) in enumerate(
            [
                (x_hbm, x_ref), (gi_hbm, gi_ref), (lengths_hbm, lengths_ref),
                (w_hbm, w_ref), (go_hbm, go_ref), (wo_hbm, wo_ref),
            ]
        )
    ]
    for load in loads:
        load.start()
    rows, cols, feat = x_ref.shape
    cols_n = chans * subs
    per_col = cols // rows
    chunks = rows // 8
    row = lax.axis_index("row")
    chan, sub = lax.axis_index("chan"), lax.axis_index("sub")
    col = chan * subs + sub

    def in_row(other):
        return {"chan": other // subs, "sub": lax.rem(other, subs)}

    up, down = lax.rem(row + 1, rows_n), lax.rem(row + rows_n - 1, rows_n)
    barrier = pltpu.get_barrier_semaphore()
    pl.semaphore_signal(barrier, inc=1, device_id={"row": down}, device_id_type=MESH)
    for t in range(1, cols_n):
        pl.semaphore_signal(
            barrier, inc=1, device_id=in_row(lax.rem(col + t, cols_n)), device_id_type=MESH
        )

    loads[2].wait()

    def positions(start, shape, axis):
        return start + lax.broadcasted_iota(jnp.int32, shape, axis)

    row_lead = valid_at(lengths_ref, positions(row * rows, (rows, 1, feat), 0), slot)
    col_lead = valid_at(lengths_ref, positions(col * cols, (cols, 1, feat), 0), slot)
    row_line = valid_at(lengths_ref, positions(row * rows, (1, rows, feat), 1), slot)
    col_line = valid_at(lengths_ref, positions(col * cols, (1, cols, feat), 1), slot)

    def edges(normed, mask, module, first):
        both = jnp.dot(
            normed, w_ref[module, :, first : first + 2 * feat], preferred_element_type=f32
        )
        return mask * jax.nn.sigmoid(both[:, feat:]) * both[:, :feat]

    def flat(values):
        return values.reshape(values.shape[0] * values.shape[1], values.shape[2])

    def copy(source, target, send, receive, device):
        return pltpu.make_async_remote_copy(
            src_ref=source, dst_ref=target, send_sem=send, recv_sem=receive,
            device_id=device, device_id_type=MESH,
        )

    loads[0].wait()
    loads[1].wait()
    source = flat(x_ref[...].astype(f32))
    normed = layer_norm(source, gi_ref[0:1, :])
    turned = flat(jnp.swapaxes(normed.reshape(rows, cols, feat), 0, 1)).astype(bf16)
    mask = flat(col_lead * row_line)
    loads[3].wait()
    right_now = edges(turned, mask, 0, 2 * feat).reshape(cols, rows, feat)
    for c in range(chunks):
        r_send[c] = flat(right_now[:, 8 * c : 8 * c + 8, :]).astype(bf16)
    pl.semaphore_wait(barrier, cols_n)

    def r_copy(origin, c, held):
        return copy(held, r_recv.at[origin, c], r_ssem.at[origin, c], r_rsem.at[origin, c], {"row": up})

    def p_copy(origin, c):
        owner, place = origin // per_col, lax.rem(origin, per_col)
        return copy(
            p_send.at[origin, c], p_recv.at[col, place, c], p_ssem.at[origin, c],
            p_rsem.at[col, place, c], in_row(owner),
        )

    def spread(origin, c, held):
        part[: cols, :, :] = held[...].astype(f32).reshape(cols, 8, feat)

        def store(i, value):
            total[8 * i : 8 * i + 8, :] = value

        partial_product(
            lambda k, i: left[k, i : i + 1, :], lambda k: part[k], cols, rows, store
        )
        owner, place = origin // per_col, lax.rem(origin, per_col)

        @pl.when(owner != col)
        def _():
            p_send[origin, c] = total[: 8 * rows, :].astype(bf16)
            p_copy(origin, c).start()

        @pl.when(owner == col)
        def _():
            p_own[place, c] = total[: 8 * rows, :]

    for c in range(chunks):
        r_copy(row, c, r_send.at[c]).start()
    left[: cols, : rows, :] = (
        edges(turned, mask, 0, 0).astype(bf16).astype(f32).reshape(cols, rows, feat)
    )
    gate[...] = jax.nn.sigmoid(
        jnp.dot(normed.astype(bf16), w_ref[0, :, 4 * feat :], preferred_element_type=f32)
    )
    for c in range(chunks):
        spread(row, c, r_send.at[c])

    def r_step(s, carry):
        origin = lax.rem(row + rows_n - s, rows_n)
        for c in range(chunks):
            held = r_recv.at[origin, c]
            r_copy(origin, c, held).wait_recv()

            @pl.when(s < rows_n - 1)
            def _():
                r_copy(origin, c, held).start()

            spread(origin, c, held)
        return carry

    lax.fori_loop(1, rows_n, r_step, 0)

    loads[4].wait()
    loads[5].wait()
    pieces = []
    for place in range(per_col):
        for c in range(chunks):
            piece = p_own[place, c]
            for t in range(1, cols_n):
                other = lax.rem(col + t, cols_n)
                copy(
                    p_send.at[0, c], p_recv.at[other, place, c], p_ssem.at[0, c],
                    p_rsem.at[other, place, c], in_row(other),
                ).wait_recv()
                piece += p_recv[other, place, c].astype(f32)
            pieces.append(piece.reshape(rows, 8, feat))
    product = flat(jnp.concatenate(pieces, axis=1))

    def finish(product, source, module):
        renormed = layer_norm(product, go_ref[module : module + 1, :]).astype(bf16)
        update = gate[...] * jnp.dot(renormed, wo_ref[module], preferred_element_type=f32)
        return (source + update).astype(bf16)

    middle = finish(product, flat(x_ref[...].astype(f32)), 0).astype(f32)
    mid[...] = middle

    normed = layer_norm(middle, gi_ref[1:2, :]).astype(bf16)
    mask = flat(row_lead * col_line)
    left_now = edges(normed, mask, 1, 0).reshape(rows, cols, feat)
    for place in range(per_col):
        for c in range(chunks):
            first = place * rows + 8 * c
            l_send[place, c] = flat(left_now[:, first : first + 8, :]).astype(bf16)

    def dest(s):
        return lax.rem(row + 2 * rows_n - 1 - s, rows_n)

    def l_copy(d, c, other):
        place = lax.rem(d, per_col)
        return copy(
            l_send.at[place, c], l_recv.at[d, c], l_ssem.at[place, c, other],
            l_rsem.at[d, c], in_row(other),
        )

    def l_start(d):
        @pl.when(d // per_col == col)
        def _():
            for c in range(chunks):
                for t in range(1, cols_n):
                    l_copy(d, c, lax.rem(col + t, cols_n)).start()

    def q_copy(d, c):
        return copy(
            q_send.at[d, c], q_recv.at[d, c], q_ssem.at[d, c], q_rsem.at[d, c], {"row": up}
        )

    l_start(dest(0))
    right[: rows, : cols, :] = (
        edges(normed, mask, 1, 2 * feat).astype(bf16).astype(f32).reshape(rows, cols, feat)
    )
    gate[...] = jax.nn.sigmoid(
        jnp.dot(normed, w_ref[1, :, 4 * feat :], preferred_element_type=f32)
    )

    def q_step(s, first_step, last_step):
        d = dest(s)
        size = 8 * cols
        for c in range(chunks):
            @pl.when(d // per_col != col)
            def _():
                l_copy(d, c, col).wait_recv()
                part[: rows, :, :] = l_recv[d, c].astype(f32).reshape(rows, 8, feat)

            @pl.when(d // per_col == col)
            def _():
                part[: rows, :, :] = (
                    l_send[lax.rem(d, per_col), c].astype(f32).reshape(rows, 8, feat)
                )

            if c == 0 and not last_step:
                l_start(dest(s + 1))

            def store(i, value):
                total[c * size + i * cols : c * size + (i + 1) * cols, :] = value

            partial_product(
                lambda k, i: part[k, i : i + 1, :], lambda k: right[k, : cols, :], rows, 8, store
            )
            here = slice(c * size, (c + 1) * size)
            if not first_step:
                q_copy(d, c).wait_recv()
            if not last_step:
                value = total[here, :]
                if not first_step:
                    value += q_recv[d, c].astype(f32)
                q_send[d, c] = value.astype(bf16)
                q_copy(d, c).start()
            else:
                total[here, :] += q_recv[d, c].astype(f32)

    q_step(0, True, False)

    def q_between(s, carry):
        q_step(s, False, False)
        return carry

    lax.fori_loop(1, rows_n - 1, q_between, 0)
    q_step(rows_n - 1, False, True)
    product = total[: rows * cols, :]
    out_ref[...] = finish(product, mid[...], 1).astype(f32).reshape(rows, cols, feat).astype(bf16)

    for c in range(chunks):
        for s in range(rows_n - 1):
            origin = lax.rem(row + rows_n - s, rows_n)
            r_copy(origin, c, r_send.at[c]).wait_send()
            q_copy(dest(s), c).wait_send()
        for place in range(per_col):
            for t in range(1, cols_n):
                l_copy(place, c, lax.rem(col + t, cols_n)).wait_send()
        for origin in range(rows_n):

            @pl.when(origin // per_col != col)
            def _():
                p_copy(origin, c).wait_send()


def solution(mesh):
    rows_n, chans, subs = mesh.shape["row"], mesh.shape["chan"], mesh.shape["sub"]
    cols_n = chans * subs

    def body(pair_state, chain_lengths, proj_weights, out_weights, input_gains, output_gains):
        rows, cols, feat = pair_state.shape
        slot = rows * rows_n // chain_lengths.shape[0]
        per_col = cols // rows
        pairs, chunks = rows * cols, rows // 8
        vmem = pl.BlockSpec(memory_space=pltpu.VMEM)
        dma = pltpu.SemaphoreType.DMA
        return pl.pallas_call(
            functools.partial(kernel, rows_n, chans, subs, slot),
            out_shape=jax.ShapeDtypeStruct(pair_state.shape, bf16),
            in_specs=[pl.BlockSpec(memory_space=pl.ANY)] * 6,
            out_specs=vmem,
            scratch_shapes=[
                pltpu.VMEM(pair_state.shape, bf16),
                pltpu.SMEM(chain_lengths.shape, jnp.int32),
                pltpu.VMEM(proj_weights.shape, bf16),
                pltpu.VMEM(out_weights.shape, bf16),
                pltpu.VMEM(input_gains.shape, f32),
                pltpu.VMEM(output_gains.shape, f32),
                dma((6,)),
                pltpu.VMEM((cols, cols, feat), f32),
                pltpu.VMEM((cols, cols, feat), f32),
                pltpu.VMEM((cols, 8, feat), f32),
                pltpu.VMEM((pairs, feat), f32),
                pltpu.VMEM((pairs, feat), f32),
                pltpu.VMEM((pairs, feat), f32),
                pltpu.VMEM((chunks, cols * 8, feat), bf16),
                pltpu.VMEM((rows_n, chunks, cols * 8, feat), bf16),
                pltpu.VMEM((rows_n, chunks, rows * 8, feat), bf16),
                pltpu.VMEM((cols_n, per_col, chunks, rows * 8, feat), bf16),
                pltpu.VMEM((per_col, chunks, rows * 8, feat), f32),
                pltpu.VMEM((per_col, chunks, rows * 8, feat), bf16),
                pltpu.VMEM((rows_n, chunks, rows * 8, feat), bf16),
                pltpu.VMEM((rows_n, chunks, cols * 8, feat), bf16),
                pltpu.VMEM((rows_n, chunks, cols * 8, feat), bf16),
                dma((rows_n, chunks)), dma((rows_n, chunks)),
                dma((rows_n, chunks)), dma((cols_n, per_col, chunks)),
                dma((per_col, chunks, cols_n)), dma((rows_n, chunks)),
                dma((rows_n, chunks)), dma((rows_n, chunks)),
            ],
            compiler_params=pltpu.CompilerParams(
                collective_id=0, has_side_effects=True, vmem_limit_bytes=60 * 1024 * 1024
            ),
        )(pair_state, chain_lengths, proj_weights, out_weights, input_gains, output_gains)

    placed = (P(("crop", "row"), ("chan", "sub"), None), P("crop"), P(), P(), P(), P())
    return jax.shard_map(
        body,
        mesh=mesh,
        in_specs=placed,
        out_specs=P(("crop", "row"), ("chan", "sub"), None),
        check_vma=False,
    )
```

```python
import functools

import jax
import jax.numpy as jnp
from jax import lax
from jax.experimental import pallas as pl
from jax.experimental.pallas import tpu as pltpu
from jax.sharding import PartitionSpec as P

MESH = pl.DeviceIdType.MESH
epsilon = 1e-05
f32 = jnp.float32
bf16 = jnp.bfloat16


def layer_norm(values, gains):
    average = jnp.mean(values, axis=-1, keepdims=True)
    centred = values - average
    variance = jnp.mean(centred * centred, axis=-1, keepdims=True)
    return centred * lax.rsqrt(variance + epsilon) * gains


def valid_at(lengths_ref, positions, slot):
    valid = jnp.zeros(positions.shape, f32)
    for chain in range(lengths_ref.shape[0]):
        first = chain * slot
        inside = (positions >= first) & (positions < first + lengths_ref[chain])
        valid = jnp.where(inside, 1.0, valid)
    return valid


def partial_product(left, right, depth, count, store):
    def step(k, sums):
        other = right(k)
        return tuple(total + left(k, i) * other for i, total in enumerate(sums))

    zero = jnp.zeros(right(0).shape, f32)
    sums = lax.fori_loop(0, depth, step, (zero,) * count, unroll=8)
    for i, total in enumerate(sums):
        store(i, total)


def kernel(
    rows_n, chans, subs, slot,
    x_hbm, lengths_hbm, w_hbm, wo_hbm, gi_hbm, go_hbm, out_ref,
    x_ref, lengths_ref, w_ref, wo_ref, gi_ref, go_ref, load_sem,
    left, right, part, gate, mid, turned_ref, normed_ref, total,
    r_send, r_recv, p_send, p_recv, p_own, l_send, l_recv, q_send, q_recv,
    r_ssem, r_rsem, p_ssem, p_rsem, l_ssem, l_rsem, q_ssem, q_rsem,
):
    loads = [
        pltpu.make_async_copy(source, target, load_sem.at[n])
        for n, (source, target) in enumerate(
            [
                (x_hbm, x_ref), (gi_hbm, gi_ref), (lengths_hbm, lengths_ref),
                (w_hbm, w_ref), (go_hbm, go_ref), (wo_hbm, wo_ref),
            ]
        )
    ]
    for load in loads:
        load.start()
    rows, cols, feat = x_ref.shape
    cols_n = chans * subs
    per_col = cols // rows
    chunks = rows // 8
    row = lax.axis_index("row")
    chan, sub = lax.axis_index("chan"), lax.axis_index("sub")
    col = chan * subs + sub

    def in_row(other):
        return {"chan": other // subs, "sub": lax.rem(other, subs)}

    up, down = lax.rem(row + 1, rows_n), lax.rem(row + rows_n - 1, rows_n)
    barrier = pltpu.get_barrier_semaphore()
    pl.semaphore_signal(barrier, inc=1, device_id={"row": down}, device_id_type=MESH)
    for t in range(1, cols_n):
        pl.semaphore_signal(
            barrier, inc=1, device_id=in_row(lax.rem(col + t, cols_n)), device_id_type=MESH
        )

    loads[2].wait()

    def positions(start, shape, axis):
        return start + lax.broadcasted_iota(jnp.int32, shape, axis)

    row_lead = valid_at(lengths_ref, positions(row * rows, (rows, 1, feat), 0), slot)
    col_lead = valid_at(lengths_ref, positions(col * cols, (cols, 1, feat), 0), slot)
    row_line = valid_at(lengths_ref, positions(row * rows, (1, rows, feat), 1), slot)
    col_line = valid_at(lengths_ref, positions(col * cols, (1, cols, feat), 1), slot)

    def edges(normed, mask, module, first):
        both = jnp.dot(
            normed, w_ref[module, :, first : first + 2 * feat], preferred_element_type=f32
        )
        return mask * jax.nn.sigmoid(both[:, feat:]) * both[:, :feat]

    def flat(values):
        return values.reshape(values.shape[0] * values.shape[1], values.shape[2])

    def copy(source, target, send, receive, device):
        return pltpu.make_async_remote_copy(
            src_ref=source, dst_ref=target, send_sem=send, recv_sem=receive,
            device_id=device, device_id_type=MESH,
        )

    def set_gate(module):
        gate[...] = jax.nn.sigmoid(
            jnp.dot(normed_ref[...], w_ref[module, :, 4 * feat :], preferred_element_type=f32)
        ).reshape(rows, cols, feat)

    def finish(product, source, gates, module):
        renormed = layer_norm(product, go_ref[module : module + 1, :]).astype(bf16)
        update = gates * jnp.dot(renormed, wo_ref[module], preferred_element_type=f32)
        return (source + update).astype(bf16)

    def r_copy(origin, c, held):
        return copy(held, r_recv.at[origin, c], r_ssem.at[origin, c], r_rsem.at[origin, c], {"row": up})

    def p_copy(origin, c):
        owner, place = origin // per_col, lax.rem(origin, per_col)
        return copy(
            p_send.at[origin, c], p_recv.at[col, place, c], p_ssem.at[origin, c],
            p_rsem.at[col, place, c], in_row(owner),
        )

    def spread(origin, c, held):
        part[: cols, :, :] = held[...].astype(f32).reshape(cols, 8, feat)

        def store(i, value):
            total[8 * i : 8 * i + 8, :] = value

        partial_product(
            lambda k, i: left[k, i : i + 1, :], lambda k: part[k], cols, rows, store
        )
        owner, place = origin // per_col, lax.rem(origin, per_col)

        @pl.when(owner != col)
        def _():
            p_send[origin, c] = total[: 8 * rows, :].astype(bf16)
            p_copy(origin, c).start()

        @pl.when(owner == col)
        def _():
            p_own[place, c] = total[: 8 * rows, :]

    loads[0].wait()
    loads[1].wait()
    turned = []
    for c in range(chunks):
        source = x_ref[8 * c : 8 * c + 8, :, :].astype(f32)
        normed = layer_norm(source, gi_ref[0:1, :])
        normed_ref[8 * cols * c : 8 * cols * (c + 1), :] = flat(normed).astype(bf16)
        turned.append(flat(jnp.swapaxes(normed, 0, 1)).astype(bf16))
        if c == 0:
            loads[3].wait()
        mask = flat(col_lead * row_line[:, 8 * c : 8 * c + 8, :])
        r_send[c] = edges(turned[c], mask, 0, 2 * feat).astype(bf16)
        if c == 0:
            pl.semaphore_wait(barrier, cols_n)
        r_copy(row, c, r_send.at[c]).start()
    for c in range(chunks):
        mask = flat(col_lead * row_line[:, 8 * c : 8 * c + 8, :])
        values = edges(turned[c], mask, 0, 0).astype(bf16).astype(f32)
        left[: cols, 8 * c : 8 * c + 8, :] = values.reshape(cols, 8, feat)
    for c in range(chunks):
        spread(row, c, r_send.at[c])
    set_gate(0)

    def r_step(s, carry):
        origin = lax.rem(row + rows_n - s, rows_n)
        for c in range(chunks):
            held = r_recv.at[origin, c]
            r_copy(origin, c, held).wait_recv()

            @pl.when(s < rows_n - 1)
            def _():
                r_copy(origin, c, held).start()

            spread(origin, c, held)
        return carry

    lax.fori_loop(1, rows_n, r_step, 0)

    loads[4].wait()
    loads[5].wait()
    def dest(s):
        return lax.rem(row + 2 * rows_n - 1 - s, rows_n)

    def l_copy(d, c, other):
        place = lax.rem(d, per_col)
        return copy(
            l_send.at[place, c], l_recv.at[d, c], l_ssem.at[place, c, other],
            l_rsem.at[d, c], in_row(other),
        )

    def l_start(d):
        @pl.when(d // per_col == col)
        def _():
            for c in range(chunks):
                for t in range(1, cols_n):
                    l_copy(d, c, lax.rem(col + t, cols_n)).start()

    def q_copy(d, c):
        return copy(
            q_send.at[d, c], q_recv.at[d, c], q_ssem.at[d, c], q_rsem.at[d, c], {"row": up}
        )

    for place in range(per_col):
        for c in range(chunks):
            piece = p_own[place, c]
            for t in range(1, cols_n):
                other = lax.rem(col + t, cols_n)
                copy(
                    p_send.at[0, c], p_recv.at[other, place, c], p_ssem.at[0, c],
                    p_rsem.at[other, place, c], in_row(other),
                ).wait_recv()
                piece += p_recv[other, place, c].astype(f32)
            first = place * rows + 8 * c
            here = slice(first, first + 8)
            source = flat(x_ref[:, here, :].astype(f32))
            middle = finish(piece, source, flat(gate[:, here, :]), 0).astype(f32)
            mid[:, here, :] = middle.reshape(rows, 8, feat)
            turned = layer_norm(middle, gi_ref[1:2, :])
            turned_ref[:, here, :] = turned.reshape(rows, 8, feat)
            turned = turned.astype(bf16)
            mask = flat(row_lead * col_line[:, here, :])
            l_send[place, c] = edges(turned, mask, 1, 0).astype(bf16)

            @pl.when(dest(0) == col * per_col + place)
            def _():
                for t in range(1, cols_n):
                    l_copy(dest(0), c, lax.rem(col + t, cols_n)).start()

            values = edges(turned, mask, 1, 2 * feat).astype(bf16).astype(f32)
            right[: rows, here, :] = values.reshape(rows, 8, feat)

    def q_step(s, first_step, last_step):
        d = dest(s)
        size = 8 * cols
        for c in range(chunks):
            @pl.when(d // per_col != col)
            def _():
                l_copy(d, c, col).wait_recv()
                part[: rows, :, :] = l_recv[d, c].astype(f32).reshape(rows, 8, feat)

            @pl.when(d // per_col == col)
            def _():
                part[: rows, :, :] = (
                    l_send[lax.rem(d, per_col), c].astype(f32).reshape(rows, 8, feat)
                )

            if c == 0 and not last_step:
                l_start(dest(s + 1))

            def store(i, value):
                total[c * size + i * cols : c * size + (i + 1) * cols, :] = value

            partial_product(
                lambda k, i: part[k, i : i + 1, :], lambda k: right[k, : cols, :], rows, 8, store
            )
            here = slice(c * size, (c + 1) * size)
            if not first_step:
                q_copy(d, c).wait_recv()
            if not last_step:
                value = total[here, :]
                if not first_step:
                    value += q_recv[d, c].astype(f32)
                q_send[d, c] = value.astype(bf16)
                q_copy(d, c).start()
            else:
                lines = slice(8 * c, 8 * c + 8)
                updated = finish(
                    total[here, :] + q_recv[d, c].astype(f32),
                    flat(mid[lines]), flat(gate[lines]), 1,
                )
                out_ref[lines] = updated.astype(f32).reshape(8, cols, feat).astype(bf16)

    q_step(0, True, False)
    normed_ref[...] = flat(turned_ref[...]).astype(bf16)
    set_gate(1)

    def q_between(s, carry):
        q_step(s, False, False)
        return carry

    lax.fori_loop(1, rows_n - 1, q_between, 0)
    q_step(rows_n - 1, False, True)
    for c in range(chunks):
        for s in range(rows_n - 1):
            origin = lax.rem(row + rows_n - s, rows_n)
            r_copy(origin, c, r_send.at[c]).wait_send()
            q_copy(dest(s), c).wait_send()
        for place in range(per_col):
            for t in range(1, cols_n):
                l_copy(place, c, lax.rem(col + t, cols_n)).wait_send()
        for origin in range(rows_n):

            @pl.when(origin // per_col != col)
            def _():
                p_copy(origin, c).wait_send()


def solution(mesh):
    rows_n, chans, subs = mesh.shape["row"], mesh.shape["chan"], mesh.shape["sub"]
    cols_n = chans * subs

    def body(pair_state, chain_lengths, proj_weights, out_weights, input_gains, output_gains):
        rows, cols, feat = pair_state.shape
        slot = rows * rows_n // chain_lengths.shape[0]
        per_col = cols // rows
        pairs, chunks = rows * cols, rows // 8
        vmem = pl.BlockSpec(memory_space=pltpu.VMEM)
        dma = pltpu.SemaphoreType.DMA
        return pl.pallas_call(
            functools.partial(kernel, rows_n, chans, subs, slot),
            out_shape=jax.ShapeDtypeStruct(pair_state.shape, bf16),
            in_specs=[pl.BlockSpec(memory_space=pl.ANY)] * 6,
            out_specs=vmem,
            scratch_shapes=[
                pltpu.VMEM(pair_state.shape, bf16),
                pltpu.SMEM(chain_lengths.shape, jnp.int32),
                pltpu.VMEM(proj_weights.shape, bf16),
                pltpu.VMEM(out_weights.shape, bf16),
                pltpu.VMEM(input_gains.shape, f32),
                pltpu.VMEM(output_gains.shape, f32),
                dma((6,)),
                pltpu.VMEM((cols, cols, feat), f32),
                pltpu.VMEM((cols, cols, feat), f32),
                pltpu.VMEM((cols, 8, feat), f32),
                pltpu.VMEM((rows, cols, feat), f32),
                pltpu.VMEM((rows, cols, feat), f32),
                pltpu.VMEM((rows, cols, feat), f32),
                pltpu.VMEM((pairs, feat), bf16),
                pltpu.VMEM((pairs, feat), f32),
                pltpu.VMEM((chunks, cols * 8, feat), bf16),
                pltpu.VMEM((rows_n, chunks, cols * 8, feat), bf16),
                pltpu.VMEM((rows_n, chunks, rows * 8, feat), bf16),
                pltpu.VMEM((cols_n, per_col, chunks, rows * 8, feat), bf16),
                pltpu.VMEM((per_col, chunks, rows * 8, feat), f32),
                pltpu.VMEM((per_col, chunks, rows * 8, feat), bf16),
                pltpu.VMEM((rows_n, chunks, rows * 8, feat), bf16),
                pltpu.VMEM((rows_n, chunks, cols * 8, feat), bf16),
                pltpu.VMEM((rows_n, chunks, cols * 8, feat), bf16),
                dma((rows_n, chunks)), dma((rows_n, chunks)),
                dma((rows_n, chunks)), dma((cols_n, per_col, chunks)),
                dma((per_col, chunks, cols_n)), dma((rows_n, chunks)),
                dma((rows_n, chunks)), dma((rows_n, chunks)),
            ],
            compiler_params=pltpu.CompilerParams(
                collective_id=0, has_side_effects=True, vmem_limit_bytes=60 * 1024 * 1024
            ),
        )(pair_state, chain_lengths, proj_weights, out_weights, input_gains, output_gains)

    placed = (P(("crop", "row"), ("chan", "sub"), None), P("crop"), P(), P(), P(), P())
    return jax.shard_map(
        body,
        mesh=mesh,
        in_specs=placed,
        out_specs=P(("crop", "row"), ("chan", "sub"), None),
        check_vma=False,
    )
```
